256 devices in a mesh: dp: 32 (over x, y, core), tensor: 8 (over z).
Axes of the slice: x: 4, y: 4, z: 8, core: 2. Of those that a mesh axis runs over, the one named last changes fastest.
Arguments:
- grad_out: bfloat16 [32768, 4608], P(('dp', 'tensor')), may hold values from -6 to 6
- attn_out: bfloat16 [32768, 2048], P('dp', 'tensor'), may hold values from -0.119628906 to 0.119628906
- out_weight: bfloat16 [2048, 4608], P('tensor'), may hold values from -0.09375 to 0.09375
- error_prev: bfloat16 [32, 2048, 4608], P('dp', 'tensor'), may hold values from -3 to 3
- q_prev: float32 [4608, 64], replicated, may hold values from -0.09375 to 0.09375
Outputs:
- grad_attn: bfloat16 [32768, 2048], P('dp', 'tensor')
- p_factor: float32 [2048, 64], P('tensor')
- q_factor: float32 [4608, 64], replicated
- error_new: bfloat16 [32, 2048, 4608], P('dp', 'tensor')
The draws below stay inside these ranges and needn't reach their ends.
All inputs are finite; a program needn't handle non-finite values.
Results may differ from the reference program's by a relative error of at most 0.014.
Values may be sent and summed in bfloat16 or wider, within the bound.
No kernel may reach another device: no remote copies, remote signals or barrier semaphores. Data moves between devices by JAX's collectives and lax.ppermute only.
A program may use at most 128 MiB of HBM per device.

```python
import jax
import jax.numpy as jnp
from jax import lax

D = 4608
RANK = 64
TOK_DEV = 128
HDIM = 2048
TOKENS = 32768
N_DP = 32
N_TENSOR = 8


def block_levels(stream_key, extent, cuts, least, high):
    factor_of = 1.0
    for dim, blocks in cuts:
        heights = jax.random.uniform(jax.random.fold_in(jax.random.fold_in(stream_key, 6), dim), (blocks,), jnp.float32, least / len(cuts), high / len(cuts))
        factor_of = factor_of * jnp.repeat(jnp.exp(heights), extent[dim] // blocks).reshape((-1,) + (1,) * (len(extent) - 1 - dim))
    return factor_of


def noise(stream_key, dims, scale, bound, cuts=(), held_as=jnp.bfloat16):
    result = jax.random.normal(stream_key, dims, jnp.float32) * scale
    if len(cuts) > 0:
        result = block_levels(stream_key, dims, cuts, -0.22, 0.18) * result
    return jnp.clip(result, min=-bound, max=bound).astype(held_as)


def setup_inputs(seed: int = 0) -> dict:
    streams_of = jax.random.split(jax.random.key(seed), 6)
    return {
        "grad_out": noise(streams_of[0], (TOKENS, D), 1.0, 6.0, ((0, 256),)),
        "attn_out": noise(streams_of[1], (TOKENS, HDIM), 0.02, 0.119628906, ((0, 32), (1, 8))),
        "out_weight": noise(streams_of[2], (HDIM, D), D ** -0.5, 0.09375, ((0, 8),)),
        "error_prev": noise(streams_of[3], (N_DP, HDIM, D), 0.5, 3.0, ((0, 32), (1, 8))),
        "q_prev": noise(streams_of[4], (D, RANK), D ** -0.5, 0.09375, (), jnp.float32),
    }


def reference(grad_out, attn_out, out_weight, error_prev, q_prev):
    grad_attn = lax.dot_general(grad_out.astype(jnp.float32), out_weight.astype(jnp.float32), (((1,), (1,)), ((), ())), preferred_element_type=jnp.float32).astype(jnp.bfloat16)
    rank_rows = TOK_DEV * N_TENSOR
    ranks = jnp.arange(N_DP, dtype=jnp.int32)

    def per_rank(index):
        start = (index * rank_rows).astype(jnp.int32)
        dy_rows = lax.dynamic_slice_in_dim(grad_out, start, rank_rows, 0)
        x_rows = lax.dynamic_slice_in_dim(attn_out, start, rank_rows, 0)
        grad_weight = lax.dot_general(x_rows.astype(jnp.float32), dy_rows.astype(jnp.float32), (((0,), (0,)), ((), ())), preferred_element_type=jnp.float32)
        return grad_weight + error_prev[index].astype(jnp.float32)
    merged = lax.map(per_rank, ranks)
    p_sum = jnp.einsum('rhd,dk->hk', merged, q_prev, precision=lax.Precision.HIGHEST)
    gram_matrix = jnp.dot(p_sum.T, p_sum, precision=lax.Precision.HIGHEST)
    lower_factor = jnp.linalg.cholesky(gram_matrix)
    p_factor = jax.scipy.linalg.solve_triangular(lower_factor, p_sum.T, lower=True).T
    q_total = jnp.einsum('rhd,hk->dk', merged, p_factor, precision=lax.Precision.HIGHEST)
    q_factor = q_total / N_DP
    approx = jnp.dot(p_factor, q_factor.T, precision=lax.Precision.HIGHEST)
    error_new = (merged - approx[None]).astype(jnp.bfloat16)
    return (grad_attn, p_factor, q_factor, error_new)
```

```python
import functools

import jax
import jax.numpy as jnp
from jax import lax
from jax.experimental import pallas as pl
from jax.experimental.pallas import tpu as pltpu
from jax.sharding import Mesh
from jax.sharding import PartitionSpec as P

D, K, NZ, NXY = 4608, 64, 8, 16
TILE = 1152
HI = lax.Precision.HIGHEST


def split3(v, axis):
    hi = lax.reduce_precision(v, 8, 7)
    rest = v - hi
    mid = lax.reduce_precision(rest, 8, 7)
    low = rest - mid
    return jnp.concatenate([hi, mid, low], axis=axis).astype(jnp.bfloat16)


def fold3(v):
    n = v.shape[0] // 3
    return v[:n] + v[n : 2 * n] + v[2 * n :]


def dot(a, b, ca, cb):
    return lax.dot_general(a, b, (((ca,), (cb,)), ((), ())), preferred_element_type=jnp.float32)


def shift(v, axis, size, by):
    return lax.ppermute(v, axis, [(i, (i + by) % size) for i in range(size)])


def everyone(v, axis, n):
    return lax.all_to_all(jnp.broadcast_to(v[None], (n,) + v.shape), axis, 0, 0)


def after(v, *others):
    return lax.optimization_barrier((v,) + others)[0]


def final_kernel(z_ref, *refs):
    blocks = refs[:15]
    a_ref, e_ref, w_ref, pf_ref, qraw_ref, linv_ref = refs[15:21]
    err_ref, grad_ref, q_ref, acc_ref = refs[21:]
    step = pl.program_id(0)
    rows = jnp.concatenate([b[...] for b in blocks], axis=0)
    qf = jnp.dot(linv_ref[...], qraw_ref[...], precision=HI, preferred_element_type=jnp.float32)
    qf = qf * (1.0 / 32)
    q_ref[...] = qf.T
    pf = pf_ref[...]
    pf_hi = pf.astype(jnp.bfloat16)
    pf_lo = (pf - pf_hi.astype(jnp.float32)).astype(jnp.bfloat16)
    q_hi = qf.astype(jnp.bfloat16)
    q_lo = (qf - q_hi.astype(jnp.float32)).astype(jnp.bfloat16)
    low = dot(
        jnp.concatenate([pf_hi, pf_hi, pf_lo], axis=0),
        jnp.concatenate([q_hi, q_lo, q_hi], axis=0), 0, 0,
    )
    fresh = jnp.dot(a_ref[...], rows, preferred_element_type=jnp.float32)
    err_ref[0] = (fresh + e_ref[0].astype(jnp.float32) - low).astype(jnp.bfloat16)
    part = dot(rows, w_ref[...], 1, 1)

    @pl.when(step == 0)
    def _():
        acc_ref[...] = part

    @pl.when(step > 0)
    def _():
        acc_ref[...] += part

    @pl.when(step == pl.num_programs(0) - 1)
    def _():
        z = z_ref[0]
        for j in range(NZ):
            src = lax.rem(z + (NZ - j), NZ)
            grad_ref[pl.ds(pl.multiple_of(src * 128, 128), 128), :] = acc_ref[
                j * 128 : (j + 1) * 128, :
            ].astype(jnp.bfloat16)


def final(z, blocks, a_rel_t, error_prev, out_weight, pf_t, q_raw, linv):
    col = lambda rows: pl.BlockSpec((rows, TILE), lambda i: (0, i))
    whole = lambda shape: pl.BlockSpec(shape, lambda i: (0,) * len(shape))
    err_spec = pl.BlockSpec((1, 256, TILE), lambda i: (0, 0, i))
    return pl.pallas_call(
        final_kernel,
        grid=(D // TILE,),
        in_specs=[pl.BlockSpec(memory_space=pltpu.SMEM)]
        + [col(b.shape[0]) for b in blocks]
        + [whole((256, 1024)), err_spec, col(256), whole((K, 256)), col(K), whole((K, K))],
        out_specs=[err_spec, whole((1024, 256)), pl.BlockSpec((TILE, K), lambda i: (i, 0))],
        out_shape=[
            jax.ShapeDtypeStruct((1, 256, D), jnp.bfloat16),
            jax.ShapeDtypeStruct((1024, 256), jnp.bfloat16),
            jax.ShapeDtypeStruct((D, K), jnp.float32),
        ],
        scratch_shapes=[pltpu.VMEM((1024, 256), jnp.float32)],
        compiler_params=pltpu.CompilerParams(vmem_limit_bytes=40 * 1024 * 1024),
        cost_estimate=pl.CostEstimate(
            flops=4 * 256 * 1024 * D, bytes_accessed=18 * 1024 * 1024, transcendentals=0
        ),
    )(z, *blocks, a_rel_t, error_prev, out_weight, pf_t, q_raw, linv)


def on_device(grad_out, attn_out, out_weight, error_prev, q_prev):
    z = lax.axis_index("z")
    core = lax.axis_index("core")
    up = lambda v: shift(v, "z", NZ, 1)
    down = lambda v: shift(v, "z", NZ, NZ - 1)
    swap = lambda v: shift(v, "core", 2, 1)

    def halves(v):
        n = v.shape[0] // 2
        first = core == 0
        return jnp.where(first, v[:n], v[n:]), jnp.where(first, v[n:], v[:n])

    def rejoin(mine):
        other = swap(mine)
        first = core == 0
        return jnp.concatenate(
            [jnp.where(first, mine, other), jnp.where(first, other, mine)], axis=0
        )

    ga, gb = grad_out[:64], grad_out[64:]
    u1a, d1a = up(ga), down(ga)
    u1b, d1b = up(gb), down(gb)

    q3 = split3(q_prev, 1)
    y_t = fold3(dot(q3, grad_out, 0, 1))
    y_all = everyone(y_t, "z", NZ)
    eq_t = fold3(dot(q3, error_prev[0], 0, 1))
    y_all = after(y_all, u1a, d1a)
    u2a, d2a = up(u1a), down(d1a)
    y_cat = y_all.transpose(1, 0, 2).reshape(K, 1024)
    p_t = fold3(dot(split3(y_cat, 0), attn_out, 1, 0)) + eq_t
    mine, other = halves(p_t)
    mine = jnp.sum(everyone(mine + swap(other), ("x", "y"), NXY), axis=0)
    mine = after(mine, u1b, d1b)
    u2b, d2b = up(u1b), down(d1b)
    p_t = rejoin(mine)

    p3 = split3(p_t, 0)
    terms = fold3(dot(p3, attn_out, 1, 1)).reshape(K, NZ, 128).transpose(1, 0, 2)
    gram = lax.dot_general(p_t, p_t, (((1,), (1,)), ((), ())), precision=HI)
    packed = jnp.concatenate([gram[:32], gram[32:]], axis=1)
    sent = jnp.concatenate([terms, jnp.broadcast_to(packed[None], (NZ, 32, 128))], axis=1)
    got = jnp.sum(lax.all_to_all(sent, "z", 0, 0), axis=0)
    got = after(got, u2a, d2a)
    u3a, d3a = up(u2a), down(d2a)
    gram = jnp.concatenate([got[K:, :K], got[K:, K:]], axis=0)
    q_t = fold3(dot(p3, error_prev[0], 1, 0)) + fold3(dot(split3(got[:K], 0), grad_out, 1, 0))

    q_t = after(q_t, u2b, d2b)
    u3b, d3b = up(u2b), down(d2b)
    mine, other = halves(q_t)
    mine = (mine + swap(other)).reshape(NXY, 2, D)
    mine = jnp.sum(lax.all_to_all(mine, ("x", "y"), 0, 0), axis=0)
    mine = after(mine, u3a, d3a)
    ufar = up(u3a)
    mine = jnp.sum(everyone(mine, "z", NZ), axis=0)
    mine = after(mine, u3b, d3b)
    dfar = down(d3b)
    mine = everyone(mine, ("x", "y"), NXY).reshape(32, D)
    q_raw = rejoin(mine)

    lower = jnp.linalg.cholesky(gram)
    linv = jax.scipy.linalg.solve_triangular(lower, jnp.eye(K, dtype=jnp.float32), lower=True)
    pf_t = jnp.dot(linv, p_t, precision=HI)

    order = (z - jnp.arange(NZ)) % NZ
    a_rel_t = attn_out.reshape(NZ, 128, 256)[order].reshape(1024, 256).T
    blocks = [grad_out, u1a, u1b, u2a, u2b, u3a, u3b, ufar, dfar, d3a, d3b, d2a, d2b, d1a, d1b]
    error_new, grad_attn, q_factor = final(
        z.astype(jnp.int32).reshape(1), blocks, a_rel_t, error_prev, out_weight, pf_t, q_raw, linv
    )
    return grad_attn, pf_t.T, q_factor, error_new


def solution(mesh):
    fine = Mesh(mesh.devices.reshape(4, 4, 2, 8), ("x", "y", "core", "z"))
    dp = ("x", "y", "core")
    in_specs = (P(dp + ("z",), None), P(dp, "z"), P("z", None), P(dp, "z", None), P())
    out_specs = (P(dp, "z"), P("z", None), P(), P(dp, "z", None))
    return jax.shard_map(
        on_device, mesh=fine, in_specs=in_specs, out_specs=out_specs, check_vma=False
    )
```

```python
import functools

import jax
import jax.numpy as jnp
from jax import lax
from jax.experimental import pallas as pl
from jax.experimental.pallas import tpu as pltpu
from jax.sharding import Mesh
from jax.sharding import PartitionSpec as P

D, K, NZ, NXY = 4608, 64, 8, 16
TILE = 1152
PIECES = 1
NT = D // TILE
HI = lax.Precision.HIGHEST
F32, BF16 = jnp.float32, jnp.bfloat16
SMEM = pl.BlockSpec(memory_space=pltpu.SMEM)


def split3(v):
    hi = v.astype(BF16)
    rest = v - hi.astype(F32)
    mid = rest.astype(BF16)
    low = (rest - mid.astype(F32)).astype(BF16)
    return jnp.concatenate([hi, mid, low], axis=0)


def fold3(v):
    n = v.shape[0] // 3
    return v[:n] + v[n : 2 * n] + v[2 * n :]


def dot(a, b, ca, cb, precision=None):
    return lax.dot_general(
        a, b, (((ca,), (cb,)), ((), ())), precision=precision, preferred_element_type=F32
    )


def whole(shape):
    return pl.BlockSpec(shape, lambda *_: (0,) * len(shape))


def out(shape, dtype=F32):
    return jax.ShapeDtypeStruct(shape, dtype)


def call(
    kernel, operands, in_specs, out_shapes, out_specs, grid=(1,), flops=0, scratch=(), mib=16,
    hbm_in=(), hbm_out=(),
):
    size = sum(v.size * v.dtype.itemsize for v in operands) + sum(
        s.size * jnp.dtype(s.dtype).itemsize for s in out_shapes
    )
    operands = [
        pltpu.with_memory_space_constraint(v, pltpu.HBM) if i in hbm_in else v
        for i, v in enumerate(operands)
    ]
    out_shapes = [
        pltpu.HBM(s.shape, s.dtype) if i in hbm_out else s for i, s in enumerate(out_shapes)
    ]
    return pl.pallas_call(
        kernel,
        grid=grid,
        in_specs=in_specs,
        out_specs=out_specs,
        out_shape=out_shapes,
        scratch_shapes=scratch,
        compiler_params=pltpu.CompilerParams(vmem_limit_bytes=mib * 1024 * 1024),
        cost_estimate=pl.CostEstimate(flops=flops, bytes_accessed=size, transcendentals=0),
    )(*operands)


def simple(kernel, operands, out_shapes, flops=0):
    specs = [SMEM if v.dtype == jnp.int32 else whole(v.shape) for v in operands]
    return call(kernel, operands, specs, out_shapes, [whole(s.shape) for s in out_shapes], flops=flops)


def rows_kernel(q_ref, g_ref, y_ref):
    y = fold3(dot(split3(q_ref[...]), g_ref[...], 1, 1))
    for j in range(NZ):
        y_ref[j] = y


def error_rows_kernel(q_ref, e_ref, a_ref, out_ref, a_t_ref):
    out_ref[...] = fold3(dot(split3(q_ref[...]), e_ref[0], 1, 1))
    a_t_ref[...] = a_ref[...].T


def pick(core_ref, a, b):
    return jnp.where(core_ref[0] == 0, a, b)


def left_kernel(core_ref, y_ref, a_ref, eq_ref, mine_ref, other_ref):
    y = jnp.concatenate([y_ref[j] for j in range(NZ)], axis=1)
    p = fold3(dot(split3(y), a_ref[...], 1, 0)) + eq_ref[...]
    mine_ref[...] = pick(core_ref, p[:32], p[32:])
    other_ref[...] = pick(core_ref, p[32:], p[:32])


def total(ref):
    acc = ref[0]
    for j in range(1, ref.shape[0]):
        acc = acc + ref[j]
    return acc


def total_kernel(in_ref, out_ref):
    out_ref[...] = total(in_ref)


def spread_kernel(in_ref, out_ref):
    acc = total(in_ref)
    for j in range(out_ref.shape[0]):
        out_ref[j] = acc


def pair_kernel(a_ref, b_ref, out_ref):
    acc = a_ref[...] + b_ref[...]
    for j in range(out_ref.shape[0]):
        out_ref[j] = acc


def add_kernel(a_ref, b_ref, out_ref):
    out_ref[...] = a_ref[...] + b_ref[...]


def terms_kernel(core_ref, mine_ref, other_ref, a_ref, p_ref, sent_ref):
    mine, other = mine_ref[...], other_ref[...]
    p = jnp.concatenate([pick(core_ref, mine, other), pick(core_ref, other, mine)], axis=0)
    p_ref[...] = p
    terms = fold3(dot(split3(p), a_ref[...], 1, 0))
    gram = dot(p, p, 1, 1, HI)
    packed = jnp.concatenate([gram[:32], gram[32:]], axis=1)
    for j in range(NZ):
        sent_ref[j, :K] = terms[:, 128 * j : 128 * (j + 1)]
        sent_ref[j, K:] = packed


def error_terms_kernel(p_ref, e_ref, out_ref):
    out_ref[...] = fold3(dot(split3(p_ref[...]), e_ref[0], 1, 0))


def right_kernel(core_ref, got_ref, ep_ref, g_ref, mine_ref, other_ref, gram_ref):
    got = total(got_ref)
    gram_ref[...] = jnp.concatenate([got[K:, :K], got[K:, K:]], axis=0)
    q = fold3(dot(split3(got[:K]), g_ref[...], 1, 0)) + ep_ref[...]
    mine_ref[:, 0] = pick(core_ref, q[:32], q[32:]).reshape(4, 8, TILE)
    other_ref[:, 0] = pick(core_ref, q[32:], q[:32]).reshape(4, 8, TILE)


def factor_kernel(gram_ref, p_ref, linv_ref, pf_ref):
    row = lax.broadcasted_iota(jnp.int32, (K, K), 0)
    lane = lax.broadcasted_iota(jnp.int32, (K, K), 1)
    eye = jnp.where(row == lane, 1.0, 0.0)
    both = jnp.concatenate([gram_ref[...], eye], axis=1)
    tiles = [both[8 * t : 8 * t + 8] for t in range(8)]
    sub = lax.broadcasted_iota(jnp.int32, (8, 128), 0)
    for i in range(K):
        b, r = divmod(i, 8)
        pivot = tiles[b][r : r + 1]
        scaled = pivot * (1.0 / pivot[:, i : i + 1])
        for t in range(b, 8):
            factor = jnp.broadcast_to(tiles[t][:, i : i + 1], (8, 128))
            if t == b:
                factor = jnp.where(sub > r, factor, 0.0)
            tiles[t] = tiles[t] - factor * scaled
    both = jnp.concatenate(tiles, axis=0)
    pivots = jnp.sum(both[:, :K] * eye, axis=1, keepdims=True)
    linv = both[:, K:] * lax.rsqrt(pivots)
    linv_ref[...] = linv
    pf_ref[...] = dot(linv, p_ref[...], 1, 0, HI)


def bulk_kernel(first, last, *refs):
    if first:
        rows_ref, a_ref, e_ref, w_ref = refs[:4]
    else:
        rows_ref, a_ref, e_ref, w_ref, sum_ref = refs[:5]
    if last:
        merged_ref, grad_ref, acc_ref = refs[-3:]
    else:
        merged_ref, acc_ref = refs[-2:]
    step = pl.program_id(0)
    rows = rows_ref[...]
    merged_ref[...] = jnp.dot(
        a_ref[...], rows, preferred_element_type=F32
    ) + e_ref[0].astype(F32)
    part = dot(rows, w_ref[...], 1, 1)

    @pl.when(step == 0)
    def _():
        acc_ref[...] = part if first else sum_ref[...] + part

    @pl.when(step > 0)
    def _():
        acc_ref[...] += part

    if last:

        @pl.when(step == pl.num_programs(0) - 1)
        def _():
            grad_ref[...] = acc_ref[...].astype(BF16)


def bulk(piece, rows, a_t, error_prev, out_weight, grad_sum):
    first, last = piece == 0, piece == PIECES - 1
    steps = rows.shape[1] // TILE
    base = piece * steps
    operands = [rows, a_t, error_prev, out_weight] + ([] if first else [grad_sum])
    specs = [
        pl.BlockSpec((1024, TILE), lambda i: (0, i)),
        whole((256, 1024)),
        pl.BlockSpec((1, 256, TILE), lambda i: (0, 0, base + i)),
        pl.BlockSpec((256, TILE), lambda i: (0, base + i)),
    ] + ([] if first else [whole((1024, 256))])
    out_shapes = [out((256, rows.shape[1])), out((1024, 256), BF16 if last else F32)]
    return call(
        functools.partial(bulk_kernel, first, last), operands, specs, out_shapes,
        [pl.BlockSpec((256, TILE), lambda i: (0, i)), whole((1024, 256))], grid=(steps,),
        flops=4 * 256 * 1024 * rows.shape[1],
        scratch=[pltpu.VMEM((1024, 256), F32)] if last else [], mib=28,
        hbm_in=(0, 1, 2, 3), hbm_out=(0, 1) if last else (0,),
    )


def tail_kernel(core_ref, mine_ref, other_ref, linv_ref, pf_ref, *refs):
    merged_refs, (err_ref, q_ref) = refs[:-2], refs[-2:]
    merged = merged_refs[-1][...]
    for piece in range(PIECES - 1):
        here = pl.program_id(0) // (NT // PIECES) == piece
        merged = jnp.where(here, merged_refs[piece][...], merged)
    mine = mine_ref[:, 0].reshape(32, TILE)
    other = other_ref[:, 0].reshape(32, TILE)
    raw = jnp.concatenate([pick(core_ref, mine, other), pick(core_ref, other, mine)], axis=0)
    qf = dot(linv_ref[...], raw, 1, 0, HI) * (1.0 / 32)
    q_ref[...] = qf
    pf = pf_ref[...]
    pf_hi = pf.astype(BF16)
    pf_lo = (pf - pf_hi.astype(F32)).astype(BF16)
    q_hi = qf.astype(BF16)
    q_lo = (qf - q_hi.astype(F32)).astype(BF16)
    low = dot(
        jnp.concatenate([pf_hi, pf_hi, pf_lo], axis=0),
        jnp.concatenate([q_hi, q_lo, q_hi], axis=0), 0, 0,
    )
    err_ref[0] = (merged - low).astype(BF16)


def shift(v, axis, size, by):
    return lax.ppermute(v, axis, [(i, (i + by) % size) for i in range(size)])


def after(v, *others):
    return lax.optimization_barrier((v,) + others)[0]


def on_device(grad_out, attn_out, out_weight, error_prev, q_prev):
    core = lax.axis_index("core").astype(jnp.int32).reshape(1)
    swap = lambda v: shift(v, "core", 2, 1)
    plane = lambda v: lax.all_to_all(v, ("x", "y"), 0, 0)
    column = lambda v: lax.all_to_all(v, "z", 0, 0)
    q_prev_t = q_prev.T
    tile = lambda rows: pl.BlockSpec((rows, TILE), lambda i: (0, i))
    err_tile = pl.BlockSpec((1, 256, TILE), lambda i: (0, 0, i))
    chunk_tile = pl.BlockSpec((4, 1, 8, TILE), lambda i: (0, i, 0, 0))
    chunks = (NXY, 8, TILE)
    width = D // PIECES
    gathered = [
        lax.all_gather(grad_out[:, i * width : (i + 1) * width], "z", axis=0, tiled=True)
        for i in range(PIECES)
    ]

    (y,) = simple(
        rows_kernel, [q_prev_t, grad_out], [out((NZ, K, 128))], flops=2 * 192 * 128 * D
    )
    y = column(y)
    eq_t, a_t = simple(
        error_rows_kernel, [q_prev_t, error_prev, attn_out],
        [out((K, 256)), out((256, 1024), BF16)], flops=2 * 192 * 256 * D,
    )
    mine, other = simple(
        left_kernel, [core, y, attn_out, eq_t], [out((32, 256)), out((32, 256))],
        flops=2 * 192 * 256 * 1024,
    )
    (mine,) = simple(pair_kernel, [mine, swap(other)], [out((NXY, 32, 256))])
    (mine,) = simple(total_kernel, [plane(mine)], [out((32, 256))])

    p_t, sent = simple(
        terms_kernel, [core, mine, swap(mine), a_t], [out((K, 256)), out((NZ, 96, 128))],
        flops=2 * 192 * 256 * 1024,
    )
    got = column(sent)
    (ep,) = call(
        error_terms_kernel, [p_t, error_prev], [whole((K, 256)), err_tile], [out((K, D))],
        [tile(K)], grid=(NT,), flops=2 * 192 * 256 * D,
    )
    mine, other, gram = call(
        right_kernel, [core, got, ep, grad_out],
        [SMEM, whole((NZ, 96, 128)), tile(K), tile(128)],
        [out((4, NT, 8, TILE)), out((4, NT, 8, TILE)), out((K, K))],
        [chunk_tile, chunk_tile, whole((K, K))], grid=(NT,), flops=2 * 192 * 128 * D,
    )

    (mine,) = simple(add_kernel, [mine.reshape(chunks), swap(other).reshape(chunks)], [out(chunks)])
    mine = plane(mine)
    linv, pf_t = simple(factor_kernel, [gram, p_t], [out((K, K)), out((K, 256))], flops=300000000)
    mine, linv, pf_t = lax.optimization_barrier((mine, linv, pf_t))
    (mine,) = simple(spread_kernel, [mine], [out((NZ, 8, TILE))])
    mine = column(mine)
    merged, grad_attn = [], None
    for piece in range(PIECES):
        if piece == PIECES - 1:
            (mine,) = simple(spread_kernel, [mine], [out(chunks)])
            mine = plane(mine)
        part, grad_attn = bulk(piece, gathered[piece], a_t, error_prev, out_weight, grad_attn)
        merged.append(part)
        mine, grad_attn, *merged = lax.optimization_barrier((mine, grad_attn, *merged))
    other = swap(mine)
    per = NT // PIECES
    slot = lambda piece: pl.BlockSpec((256, TILE), lambda i: (0, jnp.clip(i - piece * per, 0, per - 1)))
    error_new, q_t = call(
        tail_kernel,
        [core, mine.reshape(4, NT, 8, TILE), other.reshape(4, NT, 8, TILE), linv, pf_t, *merged],
        [SMEM, chunk_tile, chunk_tile, whole((K, K)), whole((K, 256))]
        + [slot(piece) for piece in range(PIECES)],
        [out((1, 256, D), BF16), out((K, D))], [err_tile, tile(K)], grid=(NT,),
        flops=2 * 256 * 192 * D, hbm_in=(5, 6), hbm_out=(0, 1),
    )
    return grad_attn, pf_t.T, q_t.T, error_new


def solution(mesh):
    fine = Mesh(mesh.devices.reshape(4, 4, 2, 8), ("x", "y", "core", "z"))
    dp = ("x", "y", "core")
    in_specs = (P(dp + ("z",), None), P(dp, "z"), P("z", None), P(dp, "z", None), P())
    out_specs = (P(dp, "z"), P("z", None), P(), P(dp, "z", None))
    return jax.shard_map(
        on_device, mesh=fine, in_specs=in_specs, out_specs=out_specs, check_vma=False
    )
```

```python
import jax
import jax.numpy as jnp
from jax import lax
from jax.experimental import pallas as pl
from jax.experimental.pallas import tpu as pltpu
from jax.sharding import Mesh
from jax.sharding import PartitionSpec as P

D, K, NZ, NXY = 4608, 64, 8, 16
TILE = 1152
FAR = (7, 8, 9, 10)
NEAR = tuple(h for h in range(16) if h not in FAR)
NT = D // TILE
HI = lax.Precision.HIGHEST
F32, BF16 = jnp.float32, jnp.bfloat16
SMEM = pl.BlockSpec(memory_space=pltpu.SMEM)


def split3(v):
    hi = v.astype(BF16)
    rest = v - hi.astype(F32)
    mid = rest.astype(BF16)
    low = (rest - mid.astype(F32)).astype(BF16)
    return jnp.concatenate([hi, mid, low], axis=0)


def fold3(v):
    n = v.shape[0] // 3
    return v[:n] + v[n : 2 * n] + v[2 * n :]


def dot(a, b, ca, cb, precision=None):
    return lax.dot_general(
        a, b, (((ca,), (cb,)), ((), ())), precision=precision, preferred_element_type=F32
    )


def whole(shape):
    return pl.BlockSpec(shape, lambda *_: (0,) * len(shape))


def out(shape, dtype=F32):
    return jax.ShapeDtypeStruct(shape, dtype)


def call(
    kernel, operands, in_specs, out_shapes, out_specs, grid=(1,), flops=0, scratch=(), mib=16,
    hbm_in=(), hbm_out=(), size=0,
):
    operands = [
        pltpu.with_memory_space_constraint(v, pltpu.HBM) if i in hbm_in else v
        for i, v in enumerate(operands)
    ]
    out_shapes = [
        pltpu.HBM(s.shape, s.dtype) if i in hbm_out else s for i, s in enumerate(out_shapes)
    ]
    return pl.pallas_call(
        kernel,
        grid=grid,
        in_specs=in_specs,
        out_specs=out_specs,
        out_shape=out_shapes,
        scratch_shapes=scratch,
        compiler_params=pltpu.CompilerParams(vmem_limit_bytes=mib * 1024 * 1024),
        cost_estimate=pl.CostEstimate(flops=flops, bytes_accessed=size, transcendentals=0),
    )(*operands)


def simple(kernel, operands, out_shapes, **kwargs):
    specs = [SMEM if v.dtype == jnp.int32 else whole(v.shape) for v in operands]
    return call(kernel, operands, specs, out_shapes, [whole(s.shape) for s in out_shapes], **kwargs)


def rows_kernel(q_ref, g_ref, y_ref, ga_ref, gb_ref, acc_ref):
    rows = g_ref[...]
    ga_ref[...] = rows[:64]
    gb_ref[...] = rows[64:]
    accumulate(acc_ref, fold3(dot(split3(q_ref[...]), rows, 1, 1)))

    @pl.when(pl.program_id(0) == pl.num_programs(0) - 1)
    def _():
        y = acc_ref[...]
        for j in range(NZ):
            y_ref[j] = y


def error_rows_kernel(q_ref, e_ref, out_ref):
    out_ref[...] = fold3(dot(split3(q_ref[...]), e_ref[0], 1, 1))


def turn_kernel(z_ref, a_ref, near_ref, far_ref):
    parts = []
    for hops in range(NZ):
        src = lax.rem(z_ref[0] + (NZ - hops), NZ)
        parts.append(a_ref[pl.ds(pl.multiple_of(src * 128, 128), 128), :].T)
    turned = jnp.concatenate(parts, axis=1)
    near_ref[...] = jnp.concatenate([turned[:, :448], turned[:, 704:]], axis=1)
    far_ref[...] = turned[:, 448:704]


def pick(core_ref, a, b):
    return jnp.where(core_ref[0] == 0, a, b)


def left_kernel(core_ref, y_ref, a_ref, eq_ref, mine_ref, other_ref):
    y = jnp.concatenate([y_ref[j] for j in range(NZ)], axis=1)
    p = fold3(dot(split3(y), a_ref[...], 1, 0)) + eq_ref[...]
    mine_ref[...] = pick(core_ref, p[:32], p[32:])
    other_ref[...] = pick(core_ref, p[32:], p[:32])


def total(ref):
    acc = ref[0]
    for j in range(1, ref.shape[0]):
        acc = acc + ref[j]
    return acc


def total_kernel(in_ref, out_ref):
    out_ref[...] = total(in_ref)


def spread_kernel(in_ref, out_ref):
    acc = total(in_ref)
    for j in range(out_ref.shape[0]):
        out_ref[j] = acc


def pair_kernel(a_ref, b_ref, out_ref):
    acc = a_ref[...] + b_ref[...]
    for j in range(out_ref.shape[0]):
        out_ref[j] = acc


def add_kernel(a_ref, b_ref, out_ref):
    out_ref[...] = a_ref[...] + b_ref[...]


def terms_kernel(core_ref, mine_ref, other_ref, a_ref, p_ref, sent_ref):
    mine, other = mine_ref[...], other_ref[...]
    p = jnp.concatenate([pick(core_ref, mine, other), pick(core_ref, other, mine)], axis=0)
    p_ref[...] = p
    terms = fold3(dot(split3(p), a_ref[...], 1, 1))
    gram = dot(p, p, 1, 1, HI)
    packed = jnp.concatenate([gram[:32], gram[32:]], axis=1)
    for j in range(NZ):
        sent_ref[j, :K] = terms[:, 128 * j : 128 * (j + 1)]
        sent_ref[j, K:] = packed


def error_terms_kernel(p_ref, e_ref, out_ref):
    out_ref[...] = fold3(dot(split3(p_ref[...]), e_ref[0], 1, 0))


def right_kernel(core_ref, got_ref, ep_ref, g_ref, mine_ref, other_ref, gram_ref):
    got = total(got_ref)
    gram_ref[...] = jnp.concatenate([got[K:, :K], got[K:, K:]], axis=0)
    q = fold3(dot(split3(got[:K]), g_ref[...], 1, 0)) + ep_ref[...]
    mine_ref[:, 0] = pick(core_ref, q[:32], q[32:]).reshape(4, 8, TILE)
    other_ref[:, 0] = pick(core_ref, q[32:], q[:32]).reshape(4, 8, TILE)


def factor_kernel(gram_ref, p_ref, linv_ref, pf_ref):
    row = lax.broadcasted_iota(jnp.int32, (K, K), 0)
    lane = lax.broadcasted_iota(jnp.int32, (K, K), 1)
    eye = jnp.where(row == lane, 1.0, 0.0)
    both = jnp.concatenate([gram_ref[...], eye], axis=1)
    tiles = [both[8 * t : 8 * t + 8] for t in range(8)]
    sub = lax.broadcasted_iota(jnp.int32, (8, 128), 0)
    for i in range(K):
        b, r = divmod(i, 8)
        pivot = tiles[b][r : r + 1]
        scaled = pivot * (1.0 / pivot[:, i : i + 1])
        for t in range(b, 8):
            factor = jnp.broadcast_to(tiles[t][:, i : i + 1], (8, 128))
            if t == b:
                factor = jnp.where(sub > r, factor, 0.0)
            tiles[t] = tiles[t] - factor * scaled
    both = jnp.concatenate(tiles, axis=0)
    pivots = jnp.sum(both[:, :K] * eye, axis=1, keepdims=True)
    linv = both[:, K:] * lax.rsqrt(pivots)
    linv_ref[...] = linv
    pf_ref[...] = dot(linv, p_ref[...], 1, 0, HI)


def place(grad_ref, z_ref, halves, acc_ref):
    for slot, half in enumerate(halves):
        src = lax.rem(z_ref[0] + (NZ - half // 2), NZ) * 128 + (half % 2) * 64
        grad_ref[pl.ds(pl.multiple_of(src, 64), 64), :] = acc_ref[
            64 * slot : 64 * (slot + 1)
        ].astype(BF16)


def accumulate(acc_ref, part):
    @pl.when(pl.program_id(0) == 0)
    def _():
        acc_ref[...] = part

    @pl.when(pl.program_id(0) > 0)
    def _():
        acc_ref[...] += part


def near_kernel(z_ref, *refs):
    blocks = refs[:-6]
    a_ref, e_ref, w_ref, merged_ref, grad_ref, acc_ref = refs[-6:]
    rows = jnp.concatenate([b[...] for b in blocks], axis=0)
    merged_ref[...] = jnp.dot(
        a_ref[...], rows, preferred_element_type=F32
    ) + e_ref[0].astype(F32)
    accumulate(acc_ref, dot(rows, w_ref[...], 1, 1))

    @pl.when(pl.program_id(0) == pl.num_programs(0) - 1)
    def _():
        place(grad_ref, z_ref, NEAR, acc_ref)


def tail_kernel(z_ref, core_ref, *refs):
    blocks = refs[:4]
    a_ref, w_ref, sum_ref, near_ref, mine_ref, other_ref, linv_ref, pf_ref = refs[4:12]
    err_ref, q_ref, grad_ref, acc_ref = refs[12:]
    mine = mine_ref[:, 0].reshape(32, TILE)
    other = other_ref[:, 0].reshape(32, TILE)
    raw = jnp.concatenate([pick(core_ref, mine, other), pick(core_ref, other, mine)], axis=0)
    qf = dot(linv_ref[...], raw, 1, 0, HI) * (1.0 / 32)
    q_ref[...] = qf
    pf = pf_ref[...]
    pf_hi = pf.astype(BF16)
    pf_lo = (pf - pf_hi.astype(F32)).astype(BF16)
    q_hi = qf.astype(BF16)
    q_lo = (qf - q_hi.astype(F32)).astype(BF16)
    low = dot(
        jnp.concatenate([pf_hi, pf_hi, pf_lo], axis=0),
        jnp.concatenate([q_hi, q_lo, q_hi], axis=0), 0, 0,
    )
    rows = jnp.concatenate([b[...] for b in blocks], axis=0)
    merged = sum_ref[...] + jnp.dot(a_ref[...], rows, preferred_element_type=F32)
    err_ref[0] = (merged - low).astype(BF16)
    accumulate(acc_ref, dot(rows, w_ref[...], 1, 1))

    @pl.when(pl.program_id(0) == pl.num_programs(0) - 1)
    def _():
        grad_ref[...] = near_ref[...]
        place(grad_ref, z_ref, FAR, acc_ref)


def shift(v, axis, size, by):
    return lax.ppermute(v, axis, [(i, (i + by) % size) for i in range(size)])


def on_device(grad_out, attn_out, out_weight, error_prev, q_prev):
    z = lax.axis_index("z").astype(jnp.int32).reshape(1)
    core = lax.axis_index("core").astype(jnp.int32).reshape(1)
    up = lambda v: shift(v, "z", NZ, 1)
    down = lambda v: shift(v, "z", NZ, NZ - 1)
    swap = lambda v: shift(v, "core", 2, 1)
    plane = lambda v: lax.all_to_all(v, ("x", "y"), 0, 0)
    column = lambda v: lax.all_to_all(v, "z", 0, 0)
    tied = lambda *v: lax.optimization_barrier(v)
    q_prev_t = q_prev.T
    tile = lambda rows: pl.BlockSpec((rows, TILE), lambda i: (0, i))
    err_tile = pl.BlockSpec((1, 256, TILE), lambda i: (0, 0, i))
    chunk_tile = pl.BlockSpec((4, 1, 8, TILE), lambda i: (0, i, 0, 0))
    chunks = (NXY, 8, TILE)

    y, ga, gb = call(
        rows_kernel, [q_prev_t, grad_out], [tile(K), tile(128)],
        [out((NZ, K, 128)), out((64, D), BF16), out((64, D), BF16)],
        [whole((NZ, K, 128)), tile(64), tile(64)], grid=(NT,),
        scratch=[pltpu.VMEM((K, 128), F32)], hbm_in=(0, 1), hbm_out=(1, 2),
    )
    y = column(y)
    (eq_t,) = simple(
        error_rows_kernel, [q_prev_t, error_prev], [out((K, 256))]
    )
    u1a, d1b = up(ga), down(gb)
    u1b, d1a = up(gb), down(ga)
    mine, other = simple(
        left_kernel, [core, y, attn_out, eq_t], [out((32, 256)), out((32, 256))]
    )
    (mine,) = simple(pair_kernel, [mine, swap(other)], [out((NXY, 32, 256))])
    mine, shadow = tied(mine, attn_out)
    mine = plane(mine)
    a_near, a_far = simple(
        turn_kernel, [z, shadow], [out((256, 768), BF16), out((256, 256), BF16)]
    )
    a_near, u1a, d1b, u1b, d1a = tied(a_near, u1a, d1b, u1b, d1a)
    u2a, d2b = up(u1a), down(d1b)
    u2b, d2a = up(u1b), down(d1a)
    mine, a_near, a_far = tied(mine, a_near, a_far)
    (mine,) = simple(total_kernel, [mine], [out((32, 256))])

    p_t, sent = simple(
        terms_kernel, [core, mine, swap(mine), attn_out], [out((K, 256)), out((NZ, 96, 128))]
    )
    got = column(sent)
    (ep,) = call(
        error_terms_kernel, [p_t, error_prev], [whole((K, 256)), err_tile], [out((K, D))],
        [tile(K)], grid=(NT,)
    )
    mine, other, gram = call(
        right_kernel, [core, got, ep, grad_out],
        [SMEM, whole((NZ, 96, 128)), tile(K), tile(128)],
        [out((4, NT, 8, TILE)), out((4, NT, 8, TILE)), out((K, K))],
        [chunk_tile, chunk_tile, whole((K, K))], grid=(NT,), hbm_in=(3,),
    )

    mine, other, u2a, d2b = tied(mine, swap(other), u2a, d2b)
    (mine,) = simple(add_kernel, [mine.reshape(chunks), other.reshape(chunks)], [out(chunks)])
    mine, gram, p_t = tied(mine, gram, p_t)
    mine = plane(mine)
    linv, pf_t = simple(factor_kernel, [gram, p_t], [out((K, K)), out((K, 256))])
    linv, u2a, d2b = tied(linv, u2a, d2b)
    u3a, d3b = up(u2a), down(d2b)
    mine, linv, pf_t = tied(mine, linv, pf_t)
    (mine,) = simple(spread_kernel, [mine], [out((NZ, 8, TILE))])
    mine, u2b, d2a = tied(mine, u2b, d2a)
    u3b, d3a = up(u2b), down(d2a)
    far_a, far_b = up(u3a), down(d3b)
    mine = column(mine)
    (mine,) = simple(spread_kernel, [mine], [out(chunks)])
    mine, a_near, u3a, d3b = tied(mine, a_near, u3a, d3b)
    mine = plane(mine)
    a_near, u3b, d3a = tied(a_near, u3b, d3a)
    near = [grad_out, u1a, u1b, u2a, u2b, u3a, d3b, d2a, d2b, d1a, d1b]
    specs = lambda blocks, a: [tile(v.shape[0]) for v in blocks] + [whole(a.shape)]
    merged, grad_near = call(
        near_kernel, [z, *near, a_near, error_prev, out_weight],
        [SMEM] + specs(near, a_near) + [err_tile, tile(256)],
        [out((256, D)), out((1024, 256), BF16)], [tile(256), whole((1024, 256))], grid=(NT,),
        scratch=[pltpu.VMEM((768, 256), F32)], mib=28,
        hbm_in=range(1, len(near) + 4), hbm_out=(0, 1),
    )
    mine, merged, grad_near = tied(mine, merged, grad_near)
    other = swap(mine)
    far = [u3b, far_a, far_b, d3a]
    error_new, q_t, grad_attn = call(
        tail_kernel,
        [z, core, *far, a_far, out_weight, merged, grad_near, mine.reshape(4, NT, 8, TILE),
         other.reshape(4, NT, 8, TILE), linv, pf_t],
        [SMEM, SMEM] + specs(far, a_far) + [tile(256), tile(256), whole((1024, 256)), chunk_tile,
         chunk_tile, whole((K, K)), whole((K, 256))],
        [out((1, 256, D), BF16), out((K, D)), out((1024, 256), BF16)],
        [err_tile, tile(K), whole((1024, 256))], grid=(NT,),
        scratch=[pltpu.VMEM((256, 256), F32)], mib=28, hbm_in=range(2, 10), hbm_out=(0, 1, 2),
    )
    return grad_attn, pf_t.T, q_t.T, error_new


def solution(mesh):
    fine = Mesh(mesh.devices.reshape(4, 4, 2, 8), ("x", "y", "core", "z"))
    dp = ("x", "y", "core")
    in_specs = (P(dp + ("z",), None), P(dp, "z"), P("z", None), P(dp, "z", None), P())
    out_specs = (P(dp, "z"), P("z", None), P(), P(dp, "z", None))
    return jax.shard_map(
        on_device, mesh=fine, in_specs=in_specs, out_specs=out_specs, check_vma=False
    )
```

```python
import jax
import jax.numpy as jnp
from jax import lax
from jax.experimental import pallas as pl
from jax.experimental.pallas import tpu as pltpu
from jax.sharding import Mesh
from jax.sharding import PartitionSpec as P

D, K, NZ, NXY = 4608, 64, 8, 16
TILE = 1152
FIRST = (0, 1, 2, 3, 14, 15)
SECOND = (4, 5, 6, 11, 12, 13)
FAR = (7, 8, 9, 10)
NT = D // TILE
HI = lax.Precision.HIGHEST
F32, BF16 = jnp.float32, jnp.bfloat16
SMEM = pl.BlockSpec(memory_space=pltpu.SMEM)


def split3(v):
    hi = v.astype(BF16)
    rest = v - hi.astype(F32)
    mid = rest.astype(BF16)
    low = (rest - mid.astype(F32)).astype(BF16)
    return jnp.concatenate([hi, mid, low], axis=0)


def fold3(v):
    n = v.shape[0] // 3
    return v[:n] + v[n : 2 * n] + v[2 * n :]


def dot(a, b, ca, cb, precision=None):
    return lax.dot_general(
        a, b, (((ca,), (cb,)), ((), ())), precision=precision, preferred_element_type=F32
    )


def whole(shape):
    return pl.BlockSpec(shape, lambda *_: (0,) * len(shape))


def out(shape, dtype=F32):
    return jax.ShapeDtypeStruct(shape, dtype)


def call(
    kernel, operands, in_specs, out_shapes, out_specs, grid=(1,), flops=0, scratch=(), mib=16,
    hbm_in=(), hbm_out=(), size=0,
):
    operands = [
        pltpu.with_memory_space_constraint(v, pltpu.HBM) if i in hbm_in else v
        for i, v in enumerate(operands)
    ]
    out_shapes = [
        pltpu.HBM(s.shape, s.dtype) if i in hbm_out else s for i, s in enumerate(out_shapes)
    ]
    return pl.pallas_call(
        kernel,
        grid=grid,
        in_specs=in_specs,
        out_specs=out_specs,
        out_shape=out_shapes,
        scratch_shapes=scratch,
        compiler_params=pltpu.CompilerParams(vmem_limit_bytes=mib * 1024 * 1024),
        cost_estimate=pl.CostEstimate(flops=flops, bytes_accessed=size, transcendentals=0),
    )(*operands)


def simple(kernel, operands, out_shapes, **kwargs):
    specs = [SMEM if v.dtype == jnp.int32 else whole(v.shape) for v in operands]
    return call(kernel, operands, specs, out_shapes, [whole(s.shape) for s in out_shapes], **kwargs)


def rows_kernel(q_ref, g_ref, y_ref, ga_ref, gb_ref, acc_ref):
    rows = g_ref[...]
    ga_ref[...] = rows[:64]
    gb_ref[...] = rows[64:]
    accumulate(acc_ref, fold3(dot(split3(q_ref[...]), rows, 1, 1)))

    @pl.when(pl.program_id(0) == pl.num_programs(0) - 1)
    def _():
        y = acc_ref[...]
        for j in range(NZ):
            y_ref[j] = y


def error_rows_kernel(q_ref, e_ref, out_ref):
    out_ref[...] = fold3(dot(split3(q_ref[...]), e_ref[0], 1, 1))


def turn_kernel(z_ref, a_ref, first_ref, second_ref, far_ref):
    parts = []
    for hops in range(NZ):
        src = lax.rem(z_ref[0] + (NZ - hops), NZ)
        parts.append(a_ref[pl.ds(pl.multiple_of(src * 128, 128), 128), :].T)
    turned = jnp.concatenate(parts, axis=1)
    first_ref[...] = jnp.concatenate([turned[:, :256], turned[:, 896:]], axis=1)
    second_ref[...] = jnp.concatenate([turned[:, 256:448], turned[:, 704:896]], axis=1)
    far_ref[...] = turned[:, 448:704]


def copy_kernel(in_ref, out_ref):
    out_ref[...] = in_ref[...]


def pick(core_ref, a, b):
    return jnp.where(core_ref[0] == 0, a, b)


def left_kernel(core_ref, y_ref, a_ref, eq_ref, mine_ref, other_ref):
    y = jnp.concatenate([y_ref[j] for j in range(NZ)], axis=1)
    p = fold3(dot(split3(y), a_ref[...], 1, 0)) + eq_ref[...]
    mine_ref[...] = pick(core_ref, p[:32], p[32:])
    other_ref[...] = pick(core_ref, p[32:], p[:32])


def total(ref):
    acc = ref[0]
    for j in range(1, ref.shape[0]):
        acc = acc + ref[j]
    return acc


def total_kernel(in_ref, out_ref):
    out_ref[...] = total(in_ref)


def spread_kernel(in_ref, out_ref):
    acc = total(in_ref)
    for j in range(out_ref.shape[0]):
        out_ref[j] = acc


def pair_kernel(a_ref, b_ref, out_ref):
    acc = a_ref[...] + b_ref[...]
    for j in range(out_ref.shape[0]):
        out_ref[j] = acc


def add_kernel(a_ref, b_ref, out_ref):
    out_ref[...] = a_ref[...] + b_ref[...]


def terms_kernel(core_ref, mine_ref, other_ref, a_ref, p_ref, sent_ref):
    mine, other = mine_ref[...], other_ref[...]
    p = jnp.concatenate([pick(core_ref, mine, other), pick(core_ref, other, mine)], axis=0)
    p_ref[...] = p
    terms = fold3(dot(split3(p), a_ref[...], 1, 1))
    gram = dot(p, p, 1, 1, HI)
    packed = jnp.concatenate([gram[:32], gram[32:]], axis=1)
    for j in range(NZ):
        sent_ref[j, :K] = terms[:, 128 * j : 128 * (j + 1)]
        sent_ref[j, K:] = packed


def error_terms_kernel(p_ref, e_ref, out_ref):
    out_ref[...] = fold3(dot(split3(p_ref[...]), e_ref[0], 1, 0))


def right_kernel(core_ref, got_ref, ep_ref, g_ref, mine_ref, other_ref, gram_ref):
    got = total(got_ref)
    gram_ref[...] = jnp.concatenate([got[K:, :K], got[K:, K:]], axis=0)
    q = fold3(dot(split3(got[:K]), g_ref[...], 1, 0)) + ep_ref[...]
    mine_ref[:, 0] = pick(core_ref, q[:32], q[32:]).reshape(4, 8, TILE)
    other_ref[:, 0] = pick(core_ref, q[32:], q[:32]).reshape(4, 8, TILE)


EARLY = 8


def eliminate(both, first, last):
    tiles = [both[8 * t : 8 * t + 8] for t in range(8)]
    sub = lax.broadcasted_iota(jnp.int32, (8, 128), 0)
    for i in range(first, last):
        b, r = divmod(i, 8)
        pivot = tiles[b][r : r + 1]
        scaled = pivot * (1.0 / pivot[:, i : i + 1])
        for t in range(b, 8):
            factor = jnp.broadcast_to(tiles[t][:, i : i + 1], (8, 128))
            if t == b:
                factor = jnp.where(sub > r, factor, 0.0)
            tiles[t] = tiles[t] - factor * scaled
    return jnp.concatenate(tiles, axis=0)


def identity():
    row = lax.broadcasted_iota(jnp.int32, (K, K), 0)
    lane = lax.broadcasted_iota(jnp.int32, (K, K), 1)
    return jnp.where(row == lane, 1.0, 0.0)


def early_kernel(gram_ref, both_ref):
    both_ref[...] = eliminate(jnp.concatenate([gram_ref[...], identity()], axis=1), 0, EARLY)


def factor_kernel(both_ref, p_ref, linv_ref, pf_ref):
    both = eliminate(both_ref[...], EARLY, K)
    pivots = jnp.sum(both[:, :K] * identity(), axis=1, keepdims=True)
    linv = both[:, K:] * lax.rsqrt(pivots)
    linv_ref[...] = linv
    pf_ref[...] = dot(linv, p_ref[...], 1, 0, HI)


def place(grad_ref, z_ref, halves, value_ref):
    for slot, half in enumerate(halves):
        src = lax.rem(z_ref[0] + (NZ - half // 2), NZ) * 128 + (half % 2) * 64
        grad_ref[pl.ds(pl.multiple_of(src, 64), 64), :] = value_ref[
            64 * slot : 64 * (slot + 1)
        ].astype(BF16)


def accumulate(acc_ref, part):
    @pl.when(pl.program_id(0) == 0)
    def _():
        acc_ref[...] = part

    @pl.when(pl.program_id(0) > 0)
    def _():
        acc_ref[...] += part


def near_kernel(*refs):
    blocks = refs[:-6]
    a_ref, w_ref, sum_ref, merged_ref, grad_ref, acc_ref = refs[-6:]
    rows = jnp.concatenate([b[...] for b in blocks], axis=0)
    before = sum_ref[...].reshape(256, TILE).astype(F32)
    merged_ref[...] = before + jnp.dot(a_ref[...], rows, preferred_element_type=F32)
    accumulate(acc_ref, dot(rows, w_ref[...], 1, 1))

    @pl.when(pl.program_id(0) == pl.num_programs(0) - 1)
    def _():
        grad_ref[...] = acc_ref[...].astype(BF16)


def tail_kernel(z_ref, core_ref, *refs):
    blocks = refs[:4]
    a_ref, w_ref, sum_ref, first_ref, second_ref, mine_ref, other_ref, linv_ref, pf_ref = refs[4:13]
    err_ref, q_ref, grad_ref, acc_ref = refs[13:]
    mine = mine_ref[:, 0].reshape(32, TILE)
    other = other_ref[:, 0].reshape(32, TILE)
    raw = jnp.concatenate([pick(core_ref, mine, other), pick(core_ref, other, mine)], axis=0)
    qf = dot(linv_ref[...], raw, 1, 0, HI) * (1.0 / 32)
    q_ref[...] = qf
    pf = pf_ref[...]
    pf_hi = pf.astype(BF16)
    pf_lo = (pf - pf_hi.astype(F32)).astype(BF16)
    q_hi = qf.astype(BF16)
    q_lo = (qf - q_hi.astype(F32)).astype(BF16)
    low = dot(
        jnp.concatenate([pf_hi, pf_hi, pf_lo], axis=0),
        jnp.concatenate([q_hi, q_lo, q_hi], axis=0), 0, 0,
    )
    rows = jnp.concatenate([b[...] for b in blocks], axis=0)
    merged = sum_ref[...] + jnp.dot(a_ref[...], rows, preferred_element_type=F32)
    err_ref[0] = (merged - low).astype(BF16)
    accumulate(acc_ref, dot(rows, w_ref[...], 1, 1))

    @pl.when(pl.program_id(0) == pl.num_programs(0) - 1)
    def _():
        place(grad_ref, z_ref, FIRST, first_ref)
        place(grad_ref, z_ref, SECOND, second_ref)
        place(grad_ref, z_ref, FAR, acc_ref)


def shift(v, axis, size, by):
    return lax.ppermute(v, axis, [(i, (i + by) % size) for i in range(size)])


def on_device(grad_out, attn_out, out_weight, error_prev, q_prev):
    z = lax.axis_index("z").astype(jnp.int32).reshape(1)
    core = lax.axis_index("core").astype(jnp.int32).reshape(1)
    up = lambda v: shift(v, "z", NZ, 1)
    down = lambda v: shift(v, "z", NZ, NZ - 1)
    swap = lambda v: shift(v, "core", 2, 1)
    plane = lambda v: lax.all_to_all(v, ("x", "y"), 0, 0)
    column = lambda v: lax.all_to_all(v, "z", 0, 0)
    tied = lambda *v: lax.optimization_barrier(v)
    q_prev_t = q_prev.T
    tile = lambda rows: pl.BlockSpec((rows, TILE), lambda i: (0, i))
    err_tile = pl.BlockSpec((1, 256, TILE), lambda i: (0, 0, i))
    chunk_tile = pl.BlockSpec((4, 1, 8, TILE), lambda i: (0, i, 0, 0))
    chunks = (NXY, 8, TILE)

    specs = lambda blocks, a: [tile(v.shape[0]) for v in blocks] + [whole(a.shape), tile(256)]

    def near(blocks, a, before, before_spec):
        return call(
            near_kernel, [*blocks, a, out_weight, before], specs(blocks, a) + [before_spec],
            [out((256, D)), out((384, 256), BF16)], [tile(256), whole((384, 256))], grid=(NT,),
            scratch=[pltpu.VMEM((384, 256), F32)], mib=28, hbm_in=range(len(blocks) + 3),
            hbm_out=(0, 1),
        )

    y, ga, gb = call(
        rows_kernel, [q_prev_t, grad_out], [tile(K), tile(128)],
        [out((NZ, K, 128)), out((64, D), BF16), out((64, D), BF16)],
        [whole((NZ, K, 128)), tile(64), tile(64)], grid=(NT,),
        scratch=[pltpu.VMEM((K, 128), F32)], hbm_in=(0, 1), hbm_out=(1, 2),
    )
    y = column(y)
    (eq_t,) = simple(error_rows_kernel, [q_prev_t, error_prev], [out((K, 256))])
    u1a, d1b = up(ga), down(gb)
    u1b, d1a = up(gb), down(ga)
    mine, other = simple(
        left_kernel, [core, y, attn_out, eq_t], [out((32, 256)), out((32, 256))]
    )
    (mine,) = simple(pair_kernel, [mine, swap(other)], [out((NXY, 32, 256))])
    mine, shadow = tied(mine, attn_out)
    mine = plane(mine)
    a_first, a_second, a_far = simple(
        turn_kernel, [z, shadow],
        [out((256, 384), BF16), out((256, 384), BF16), out((256, 256), BF16)],
    )
    a_first, u1a, d1b, u1b, d1a = tied(a_first, u1a, d1b, u1b, d1a)
    u2a, d2b = up(u1a), down(d1b)
    u2b, d2a = up(u1b), down(d1a)
    mine, a_first, a_second, a_far = tied(mine, a_first, a_second, a_far)
    (mine,) = simple(total_kernel, [mine], [out((32, 256))])

    p_t, sent = simple(
        terms_kernel, [core, mine, swap(mine), attn_out], [out((K, 256)), out((NZ, 96, 128))]
    )
    sent, p_t, a_first = tied(sent, p_t, a_first)
    got = column(sent)
    merged, grad_first = near([grad_out, u1a, u1b, d1a, d1b], a_first, error_prev, err_tile)
    p_then, u2a, d2b = tied(p_t, u2a, d2b)
    (ep,) = call(
        error_terms_kernel, [p_then, error_prev], [whole((K, 256)), err_tile], [out((K, D))],
        [tile(K)], grid=(NT,), flops=3 * 10**9,
    )
    got, merged, grad_first = tied(got, merged, grad_first)
    mine, other, gram = call(
        right_kernel, [core, got, ep, grad_out],
        [SMEM, whole((NZ, 96, 128)), tile(K), tile(128)],
        [out((4, NT, 8, TILE)), out((4, NT, 8, TILE)), out((K, K))],
        [chunk_tile, chunk_tile, whole((K, K))], grid=(NT,), hbm_in=(3,),
    )

    other = swap(other)
    (mine,) = simple(add_kernel, [mine.reshape(chunks), other.reshape(chunks)], [out(chunks)])
    mine, gram, p_t = tied(mine, gram, p_t)
    mine = plane(mine)
    (early,) = simple(early_kernel, [gram], [out((K, 128))])
    early, u2a, d2b = tied(early, u2a, d2b)
    u3a, d3b = up(u2a), down(d2b)
    linv, pf_t = simple(factor_kernel, [early, p_t], [out((K, K)), out((K, 256))])
    mine, linv, pf_t = tied(mine, linv, pf_t)
    (mine,) = simple(spread_kernel, [mine], [out((NZ, 8, TILE))])
    mine, u2b, d2a = tied(mine, u2b, d2a)
    mine = column(mine)
    u3b, d3a = up(u2b), down(d2a)
    far_a, far_b = up(u3a), down(d3b)
    (mine,) = simple(spread_kernel, [mine], [out(chunks)])
    mine, a_second, a_far, merged = tied(mine, a_second, a_far, merged)
    mine = plane(mine)
    merged, grad_second = near([u2a, u2b, u3a, d3b, d2a, d2b], a_second, merged, tile(256))
    a_far, merged, u3b, far_a, far_b, d3a = tied(a_far, merged, u3b, far_a, far_b, d3a)
    (a_far,) = simple(copy_kernel, [a_far], [out((256, 256), BF16)])
    mine, a_far, merged, grad_second = tied(mine, a_far, merged, grad_second)
    other = swap(mine)
    far = [u3b, far_a, far_b, d3a]
    error_new, q_t, grad_attn = call(
        tail_kernel,
        [z, core, *far, a_far, out_weight, merged, grad_first, grad_second,
         mine.reshape(4, NT, 8, TILE), other.reshape(4, NT, 8, TILE), linv, pf_t],
        [SMEM, SMEM] + specs(far, a_far) + [tile(256), whole((384, 256)), whole((384, 256)),
         chunk_tile, chunk_tile, whole((K, K)), whole((K, 256))],
        [out((1, 256, D), BF16), out((K, D)), out((1024, 256), BF16)],
        [err_tile, tile(K), whole((1024, 256))], grid=(NT,),
        scratch=[pltpu.VMEM((256, 256), F32)], mib=28, hbm_in=range(2, 11), hbm_out=(0, 1, 2),
    )
    return grad_attn, pf_t.T, q_t.T, error_new


def solution(mesh):
    fine = Mesh(mesh.devices.reshape(4, 4, 2, 8), ("x", "y", "core", "z"))
    dp = ("x", "y", "core")
    in_specs = (P(dp + ("z",), None), P(dp, "z"), P("z", None), P(dp, "z", None), P())
    out_specs = (P(dp, "z"), P("z", None), P(), P(dp, "z", None))
    return jax.shard_map(
        on_device, mesh=fine, in_specs=in_specs, out_specs=out_specs, check_vma=False
    )
```

```python
import jax
import jax.numpy as jnp
from jax import lax
from jax.experimental import pallas as pl
from jax.experimental.pallas import tpu as pltpu
from jax.sharding import Mesh
from jax.sharding import PartitionSpec as P

D, K, NZ, NXY = 4608, 64, 8, 16
TILE = 1152
FIRST = (0, 1, 2, 3, 14, 15)
SECOND = (4, 5, 6, 11, 12, 13)
FAR = (7, 8, 9, 10)
NT = D // TILE
HI = lax.Precision.HIGHEST
F32, BF16 = jnp.float32, jnp.bfloat16
SMEM = pl.BlockSpec(memory_space=pltpu.SMEM)


def split3(v):
    hi = v.astype(BF16)
    rest = v - hi.astype(F32)
    mid = rest.astype(BF16)
    low = (rest - mid.astype(F32)).astype(BF16)
    return jnp.concatenate([hi, mid, low], axis=0)


def fold3(v):
    n = v.shape[0] // 3
    return v[:n] + v[n : 2 * n] + v[2 * n :]


def dot(a, b, ca, cb, precision=None):
    return lax.dot_general(
        a, b, (((ca,), (cb,)), ((), ())), precision=precision, preferred_element_type=F32
    )


def whole(shape):
    return pl.BlockSpec(shape, lambda *_: (0,) * len(shape))


def out(shape, dtype=F32):
    return jax.ShapeDtypeStruct(shape, dtype)


def call(
    kernel, operands, in_specs, out_shapes, out_specs, grid=(1,), flops=0, scratch=(), mib=16,
    hbm_in=(), hbm_out=(), size=0,
):
    operands = [
        pltpu.with_memory_space_constraint(v, pltpu.HBM) if i in hbm_in else v
        for i, v in enumerate(operands)
    ]
    out_shapes = [
        pltpu.HBM(s.shape, s.dtype) if i in hbm_out else s for i, s in enumerate(out_shapes)
    ]
    return pl.pallas_call(
        kernel,
        grid=grid,
        in_specs=in_specs,
        out_specs=out_specs,
        out_shape=out_shapes,
        scratch_shapes=scratch,
        compiler_params=pltpu.CompilerParams(vmem_limit_bytes=mib * 1024 * 1024),
        cost_estimate=pl.CostEstimate(flops=flops, bytes_accessed=size, transcendentals=0),
    )(*operands)


def simple(kernel, operands, out_shapes, **kwargs):
    specs = [SMEM if v.dtype == jnp.int32 else whole(v.shape) for v in operands]
    return call(kernel, operands, specs, out_shapes, [whole(s.shape) for s in out_shapes], **kwargs)


def halves_kernel(g_ref, ga_ref, gb_ref):
    ga_ref[...] = g_ref[:64]
    gb_ref[...] = g_ref[64:]


def rows_kernel(q_ref, g_ref, y_ref, acc_ref):
    accumulate(acc_ref, fold3(dot(split3(q_ref[...]), g_ref[...], 1, 1)))

    @pl.when(pl.program_id(0) == pl.num_programs(0) - 1)
    def _():
        y = acc_ref[...]
        for j in range(NZ):
            y_ref[j] = y


def error_rows_kernel(q_ref, e_ref, out_ref):
    out_ref[...] = fold3(dot(split3(q_ref[...]), e_ref[0], 1, 1))


def turn_kernel(z_ref, a_ref, first_ref, second_ref, far_ref):
    parts = []
    for hops in range(NZ):
        src = lax.rem(z_ref[0] + (NZ - hops), NZ)
        parts.append(a_ref[pl.ds(pl.multiple_of(src * 128, 128), 128), :].T)
    turned = jnp.concatenate(parts, axis=1)
    first_ref[...] = jnp.concatenate([turned[:, :256], turned[:, 896:]], axis=1)
    second_ref[...] = jnp.concatenate([turned[:, 256:448], turned[:, 704:896]], axis=1)
    far_ref[...] = turned[:, 448:704]


def copy_kernel(in_ref, out_ref):
    out_ref[...] = in_ref[...]


def pick(core_ref, a, b):
    return jnp.where(core_ref[0] == 0, a, b)


def left_kernel(core_ref, y_ref, a_ref, eq_ref, mine_ref, other_ref):
    y = jnp.concatenate([y_ref[j] for j in range(NZ)], axis=1)
    p = fold3(dot(split3(y), a_ref[...], 1, 0)) + eq_ref[...]
    mine_ref[...] = pick(core_ref, p[:32], p[32:])
    other_ref[...] = pick(core_ref, p[32:], p[:32])


def total(ref):
    acc = ref[0]
    for j in range(1, ref.shape[0]):
        acc = acc + ref[j]
    return acc


def total_kernel(in_ref, out_ref):
    out_ref[...] = total(in_ref)


def spread_kernel(in_ref, out_ref):
    acc = total(in_ref)
    for j in range(out_ref.shape[0]):
        out_ref[j] = acc


def pair_kernel(a_ref, b_ref, out_ref):
    acc = a_ref[...] + b_ref[...]
    for j in range(out_ref.shape[0]):
        out_ref[j] = acc


def add_kernel(a_ref, b_ref, out_ref):
    out_ref[...] = a_ref[...] + b_ref[...]


def terms_kernel(core_ref, mine_ref, other_ref, a_ref, p_ref, sent_ref):
    mine, other = mine_ref[...], other_ref[...]
    p = jnp.concatenate([pick(core_ref, mine, other), pick(core_ref, other, mine)], axis=0)
    p_ref[...] = p
    terms = fold3(dot(split3(p), a_ref[...], 1, 1))
    gram = dot(p, p, 1, 1, HI)
    packed = jnp.concatenate([gram[:32], gram[32:]], axis=1)
    for j in range(NZ):
        sent_ref[j, :K] = terms[:, 128 * j : 128 * (j + 1)]
        sent_ref[j, K:] = packed


def error_terms_kernel(p_ref, e_ref, out_ref):
    out_ref[...] = fold3(dot(split3(p_ref[...]), e_ref[0], 1, 0))


def right_kernel(core_ref, got_ref, ep_ref, g_ref, mine_ref, other_ref, gram_ref):
    got = total(got_ref)
    gram_ref[...] = jnp.concatenate([got[K:, :K], got[K:, K:]], axis=0)
    q = fold3(dot(split3(got[:K]), g_ref[...], 1, 0)) + ep_ref[...]
    mine_ref[:, 0] = pick(core_ref, q[:32], q[32:]).reshape(4, 8, TILE)
    other_ref[:, 0] = pick(core_ref, q[32:], q[:32]).reshape(4, 8, TILE)


EARLY = 8


def eliminate(both, first, last):
    tiles = [both[8 * t : 8 * t + 8] for t in range(8)]
    sub = lax.broadcasted_iota(jnp.int32, (8, 128), 0)
    for i in range(first, last):
        b, r = divmod(i, 8)
        pivot = tiles[b][r : r + 1]
        scaled = pivot * (1.0 / pivot[:, i : i + 1])
        for t in range(b, 8):
            factor = jnp.broadcast_to(tiles[t][:, i : i + 1], (8, 128))
            if t == b:
                factor = jnp.where(sub > r, factor, 0.0)
            tiles[t] = tiles[t] - factor * scaled
    return jnp.concatenate(tiles, axis=0)


def identity():
    row = lax.broadcasted_iota(jnp.int32, (K, K), 0)
    lane = lax.broadcasted_iota(jnp.int32, (K, K), 1)
    return jnp.where(row == lane, 1.0, 0.0)


def early_kernel(gram_ref, both_ref):
    both_ref[...] = eliminate(jnp.concatenate([gram_ref[...], identity()], axis=1), 0, EARLY)


def factor_kernel(both_ref, p_ref, linv_ref, pf_ref):
    both = eliminate(both_ref[...], EARLY, K)
    pivots = jnp.sum(both[:, :K] * identity(), axis=1, keepdims=True)
    linv = both[:, K:] * lax.rsqrt(pivots)
    linv_ref[...] = linv
    pf_ref[...] = dot(linv, p_ref[...], 1, 0, HI)


def place(grad_ref, z_ref, halves, value_ref):
    for slot, half in enumerate(halves):
        src = lax.rem(z_ref[0] + (NZ - half // 2), NZ) * 128 + (half % 2) * 64
        grad_ref[pl.ds(pl.multiple_of(src, 64), 64), :] = value_ref[
            64 * slot : 64 * (slot + 1)
        ].astype(BF16)


def accumulate(acc_ref, part):
    @pl.when(pl.program_id(0) == 0)
    def _():
        acc_ref[...] = part

    @pl.when(pl.program_id(0) > 0)
    def _():
        acc_ref[...] += part


def near_kernel(*refs):
    blocks = refs[:-6]
    a_ref, w_ref, sum_ref, merged_ref, grad_ref, acc_ref = refs[-6:]
    rows = jnp.concatenate([b[...] for b in blocks], axis=0)
    before = sum_ref[...].reshape(256, TILE).astype(F32)
    merged_ref[...] = before + jnp.dot(a_ref[...], rows, preferred_element_type=F32)
    accumulate(acc_ref, dot(rows, w_ref[...], 1, 1))

    @pl.when(pl.program_id(0) == pl.num_programs(0) - 1)
    def _():
        grad_ref[...] = acc_ref[...].astype(BF16)


def tail_kernel(z_ref, core_ref, *refs):
    blocks = refs[:4]
    a_ref, w_ref, sum_ref, first_ref, second_ref, mine_ref, other_ref, linv_ref, pf_ref = refs[4:13]
    err_ref, q_ref, grad_ref, acc_ref = refs[13:]
    mine = mine_ref[:, 0].reshape(32, TILE)
    other = other_ref[:, 0].reshape(32, TILE)
    raw = jnp.concatenate([pick(core_ref, mine, other), pick(core_ref, other, mine)], axis=0)
    qf = dot(linv_ref[...], raw, 1, 0, HI) * (1.0 / 32)
    q_ref[...] = qf
    pf = pf_ref[...]
    pf_hi = pf.astype(BF16)
    pf_lo = (pf - pf_hi.astype(F32)).astype(BF16)
    q_hi = qf.astype(BF16)
    q_lo = (qf - q_hi.astype(F32)).astype(BF16)
    low = dot(
        jnp.concatenate([pf_hi, pf_hi, pf_lo], axis=0),
        jnp.concatenate([q_hi, q_lo, q_hi], axis=0), 0, 0,
    )
    rows = jnp.concatenate([b[...] for b in blocks], axis=0)
    merged = sum_ref[...] + jnp.dot(a_ref[...], rows, preferred_element_type=F32)
    err_ref[0] = (merged - low).astype(BF16)
    accumulate(acc_ref, dot(rows, w_ref[...], 1, 1))

    @pl.when(pl.program_id(0) == pl.num_programs(0) - 1)
    def _():
        place(grad_ref, z_ref, FIRST, first_ref)
        place(grad_ref, z_ref, SECOND, second_ref)
        place(grad_ref, z_ref, FAR, acc_ref)


def shift(v, axis, size, by):
    return lax.ppermute(v, axis, [(i, (i + by) % size) for i in range(size)])


def on_device(grad_out, attn_out, out_weight, error_prev, q_prev):
    z = lax.axis_index("z").astype(jnp.int32).reshape(1)
    core = lax.axis_index("core").astype(jnp.int32).reshape(1)
    up = lambda v: shift(v, "z", NZ, 1)
    down = lambda v: shift(v, "z", NZ, NZ - 1)
    swap = lambda v: shift(v, "core", 2, 1)
    plane = lambda v: lax.all_to_all(v, ("x", "y"), 0, 0)
    column = lambda v: lax.all_to_all(v, "z", 0, 0)
    tied = lambda *v: lax.optimization_barrier(v)
    q_prev_t = q_prev.T
    tile = lambda rows: pl.BlockSpec((rows, TILE), lambda i: (0, i))
    err_tile = pl.BlockSpec((1, 256, TILE), lambda i: (0, 0, i))
    chunk_tile = pl.BlockSpec((4, 1, 8, TILE), lambda i: (0, i, 0, 0))
    chunks = (NXY, 8, TILE)

    specs = lambda blocks, a: [tile(v.shape[0]) for v in blocks] + [whole(a.shape), tile(256)]

    def near(blocks, a, before, before_spec):
        return call(
            near_kernel, [*blocks, a, out_weight, before], specs(blocks, a) + [before_spec],
            [out((256, D)), out((384, 256), BF16)], [tile(256), whole((384, 256))], grid=(NT,),
            scratch=[pltpu.VMEM((384, 256), F32)], mib=28, hbm_in=range(len(blocks) + 3),
            hbm_out=(0, 1),
        )

    (y,) = call(
        rows_kernel, [q_prev_t, grad_out], [tile(K), tile(128)], [out((NZ, K, 128))],
        [whole((NZ, K, 128))], grid=(NT,), scratch=[pltpu.VMEM((K, 128), F32)], hbm_in=(0, 1),
        hbm_out=(0,),
    )
    ga, gb = call(
        halves_kernel, [grad_out], [tile(128)], [out((64, D), BF16)] * 2, [tile(64)] * 2,
        grid=(NT,), hbm_in=(0,), hbm_out=(0, 1),
    )
    y = column(y)
    (eq_t,) = simple(error_rows_kernel, [q_prev_t, error_prev], [out((K, 256))], hbm_out=(0,))
    u1a, d1b = up(ga), down(gb)
    u1b, d1a = up(gb), down(ga)
    mine, other = simple(
        left_kernel, [core, y, attn_out, eq_t], [out((32, 256)), out((32, 256))], hbm_in=(2, 3)
    )
    (mine,) = simple(pair_kernel, [mine, swap(other)], [out((NXY, 32, 256))])
    mine, shadow = tied(mine, attn_out)
    mine = plane(mine)
    a_first, a_second, a_far = simple(
        turn_kernel, [z, shadow],
        [out((256, 384), BF16), out((256, 384), BF16), out((256, 256), BF16)],
    )
    a_first, u1a, d1b, u1b, d1a = tied(a_first, u1a, d1b, u1b, d1a)
    u2a, d2b = up(u1a), down(d1b)
    u2b, d2a = up(u1b), down(d1a)
    mine, a_first, a_second, a_far = tied(mine, a_first, a_second, a_far)
    (mine,) = simple(total_kernel, [mine], [out((32, 256))])

    p_t, sent = simple(
        terms_kernel, [core, mine, swap(mine), attn_out], [out((K, 256)), out((NZ, 96, 128))]
    )
    sent, p_t, a_first = tied(sent, p_t, a_first)
    got = column(sent)
    merged, grad_first = near([grad_out, u1a, u1b, d1a, d1b], a_first, error_prev, err_tile)
    p_then, u2a, d2b = tied(p_t, u2a, d2b)
    (ep,) = call(
        error_terms_kernel, [p_then, error_prev], [whole((K, 256)), err_tile], [out((K, D))],
        [tile(K)], grid=(NT,), flops=3 * 10**9,
    )
    got, merged, grad_first = tied(got, merged, grad_first)
    mine, other, gram = call(
        right_kernel, [core, got, ep, grad_out],
        [SMEM, whole((NZ, 96, 128)), tile(K), tile(128)],
        [out((4, NT, 8, TILE)), out((4, NT, 8, TILE)), out((K, K))],
        [chunk_tile, chunk_tile, whole((K, K))], grid=(NT,), hbm_in=(3,),
    )

    other = swap(other)
    (mine,) = simple(add_kernel, [mine.reshape(chunks), other.reshape(chunks)], [out(chunks)])
    mine, gram, p_t = tied(mine, gram, p_t)
    mine = plane(mine)
    (early,) = simple(early_kernel, [gram], [out((K, 128))])
    early, u2a, d2b = tied(early, u2a, d2b)
    u3a, d3b = up(u2a), down(d2b)
    linv, pf_t = simple(factor_kernel, [early, p_t], [out((K, K)), out((K, 256))])
    mine, linv, pf_t = tied(mine, linv, pf_t)
    (mine,) = simple(spread_kernel, [mine], [out((NZ, 8, TILE))])
    mine, u2b, d2a = tied(mine, u2b, d2a)
    mine = column(mine)
    u3b, d3a = up(u2b), down(d2a)
    far_a, far_b = up(u3a), down(d3b)
    (mine,) = simple(spread_kernel, [mine], [out(chunks)])
    mine, a_second, a_far, merged = tied(mine, a_second, a_far, merged)
    mine = plane(mine)
    merged, grad_second = near([u2a, u2b, u3a, d3b, d2a, d2b], a_second, merged, tile(256))
    linv, merged, u3b, far_a, far_b, d3a = tied(linv, merged, u3b, far_a, far_b, d3a)
    (linv,) = simple(copy_kernel, [linv], [out((K, K))])
    mine, linv, merged, grad_second = tied(mine, linv, merged, grad_second)
    other = swap(mine)
    far = [u3b, far_a, far_b, d3a]
    error_new, q_t, grad_attn = call(
        tail_kernel,
        [z, core, *far, a_far, out_weight, merged, grad_first, grad_second,
         mine.reshape(4, NT, 8, TILE), other.reshape(4, NT, 8, TILE), linv, pf_t],
        [SMEM, SMEM] + specs(far, a_far) + [tile(256), whole((384, 256)), whole((384, 256)),
         chunk_tile, chunk_tile, whole((K, K)), whole((K, 256))],
        [out((1, 256, D), BF16), out((K, D)), out((1024, 256), BF16)],
        [err_tile, tile(K), whole((1024, 256))], grid=(NT,),
        scratch=[pltpu.VMEM((256, 256), F32)], mib=28, hbm_in=range(2, 11), hbm_out=(0, 1, 2),
    )
    return grad_attn, pf_t.T, q_t.T, error_new


def solution(mesh):
    fine = Mesh(mesh.devices.reshape(4, 4, 2, 8), ("x", "y", "core", "z"))
    dp = ("x", "y", "core")
    in_specs = (P(dp + ("z",), None), P(dp, "z"), P("z", None), P(dp, "z", None), P())
    out_specs = (P(dp, "z"), P("z", None), P(), P(dp, "z", None))
    return jax.shard_map(
        on_device, mesh=fine, in_specs=in_specs, out_specs=out_specs, check_vma=False
    )
```

```python
import jax
import jax.numpy as jnp
from jax import lax
from jax.experimental import pallas as pl
from jax.experimental.pallas import tpu as pltpu
from jax.sharding import Mesh
from jax.sharding import PartitionSpec as P

D, K, NZ, NXY = 4608, 64, 8, 16
TILE = 1152
FIRST = (0, 1, 2, 3, 14, 15)
SECOND = (4, 5, 6, 11, 12, 13)
FAR = (7, 8, 9, 10)
NT = D // TILE
HI = lax.Precision.HIGHEST
F32, BF16 = jnp.float32, jnp.bfloat16
SMEM = pl.BlockSpec(memory_space=pltpu.SMEM)


def split3(v):
    hi = v.astype(BF16)
    rest = v - hi.astype(F32)
    mid = rest.astype(BF16)
    low = (rest - mid.astype(F32)).astype(BF16)
    return jnp.concatenate([hi, mid, low], axis=0)


def fold3(v):
    n = v.shape[0] // 3
    return v[:n] + v[n : 2 * n] + v[2 * n :]


def dot(a, b, ca, cb, precision=None):
    return lax.dot_general(
        a, b, (((ca,), (cb,)), ((), ())), precision=precision, preferred_element_type=F32
    )


def whole(shape):
    return pl.BlockSpec(shape, lambda *_: (0,) * len(shape))


def out(shape, dtype=F32):
    return jax.ShapeDtypeStruct(shape, dtype)


def call(
    kernel, operands, in_specs, out_shapes, out_specs, grid=(1,), flops=0, scratch=(), mib=16,
    hbm_in=(), hbm_out=(), size=0,
):
    operands = [
        pltpu.with_memory_space_constraint(v, pltpu.HBM) if i in hbm_in else v
        for i, v in enumerate(operands)
    ]
    out_shapes = [
        pltpu.HBM(s.shape, s.dtype) if i in hbm_out else s for i, s in enumerate(out_shapes)
    ]
    return pl.pallas_call(
        kernel,
        grid=grid,
        in_specs=in_specs,
        out_specs=out_specs,
        out_shape=out_shapes,
        scratch_shapes=scratch,
        compiler_params=pltpu.CompilerParams(vmem_limit_bytes=mib * 1024 * 1024),
        cost_estimate=pl.CostEstimate(flops=flops, bytes_accessed=size, transcendentals=0),
    )(*operands)


def simple(kernel, operands, out_shapes, **kwargs):
    specs = [SMEM if v.dtype == jnp.int32 else whole(v.shape) for v in operands]
    return call(kernel, operands, specs, out_shapes, [whole(s.shape) for s in out_shapes], **kwargs)


def halves_kernel(g_ref, ga_ref, gb_ref):
    ga_ref[...] = g_ref[:64]
    gb_ref[...] = g_ref[64:]


def rows_kernel(q_ref, g_ref, y_ref, acc_ref):
    accumulate(acc_ref, fold3(dot(split3(q_ref[...]), g_ref[...], 1, 1)))

    @pl.when(pl.program_id(0) == pl.num_programs(0) - 1)
    def _():
        y = acc_ref[...]
        for j in range(NZ):
            y_ref[j] = y


def error_rows_kernel(q_ref, e_ref, out_ref):
    out_ref[...] = fold3(dot(split3(q_ref[...]), e_ref[0], 1, 1))


def turn_kernel(z_ref, a_ref, first_ref, second_ref, far_ref):
    parts = []
    for hops in range(NZ):
        src = lax.rem(z_ref[0] + (NZ - hops), NZ)
        parts.append(a_ref[pl.ds(pl.multiple_of(src * 128, 128), 128), :].T)
    turned = jnp.concatenate(parts, axis=1)
    first_ref[...] = jnp.concatenate([turned[:, :256], turned[:, 896:]], axis=1)
    second_ref[...] = jnp.concatenate([turned[:, 256:448], turned[:, 704:896]], axis=1)
    far_ref[...] = turned[:, 448:704]


def copy_kernel(in_ref, out_ref):
    out_ref[...] = in_ref[...]


def pick(core_ref, a, b):
    return jnp.where(core_ref[0] == 0, a, b)


def left_kernel(core_ref, y_ref, a_ref, eq_ref, mine_ref, other_ref):
    y = jnp.concatenate([y_ref[j] for j in range(NZ)], axis=1)
    p = fold3(dot(split3(y), a_ref[...], 1, 0)) + eq_ref[...]
    mine_ref[...] = pick(core_ref, p[:32], p[32:])
    other_ref[...] = pick(core_ref, p[32:], p[:32])


def total(ref):
    acc = ref[0]
    for j in range(1, ref.shape[0]):
        acc = acc + ref[j]
    return acc


def total_kernel(in_ref, out_ref):
    out_ref[...] = total(in_ref)


def spread_kernel(in_ref, out_ref):
    acc = total(in_ref)
    for j in range(out_ref.shape[0]):
        out_ref[j] = acc


def pair_kernel(a_ref, b_ref, out_ref):
    acc = a_ref[...] + b_ref[...]
    for j in range(out_ref.shape[0]):
        out_ref[j] = acc


def add_kernel(a_ref, b_ref, out_ref):
    out_ref[...] = a_ref[...] + b_ref[...]


def terms_kernel(core_ref, mine_ref, other_ref, a_ref, p_ref, sent_ref):
    mine, other = mine_ref[...], other_ref[...]
    p = jnp.concatenate([pick(core_ref, mine, other), pick(core_ref, other, mine)], axis=0)
    p_ref[...] = p
    terms = fold3(dot(split3(p), a_ref[...], 1, 1))
    gram = dot(p, p, 1, 1, HI)
    packed = jnp.concatenate([gram[:32], gram[32:]], axis=1)
    for j in range(NZ):
        sent_ref[j, :K] = terms[:, 128 * j : 128 * (j + 1)]
        sent_ref[j, K:] = packed


def error_terms_kernel(p_ref, e_ref, out_ref):
    out_ref[...] = fold3(dot(split3(p_ref[...]), e_ref[0], 1, 0))


def right_kernel(core_ref, got_ref, ep_ref, g_ref, mine_ref, other_ref, gram_ref):
    got = total(got_ref)
    gram_ref[...] = jnp.concatenate([got[K:, :K], got[K:, K:]], axis=0)
    q = fold3(dot(split3(got[:K]), g_ref[...], 1, 0)) + ep_ref[...]
    mine_ref[:, 0] = pick(core_ref, q[:32], q[32:]).reshape(4, 8, TILE)
    other_ref[:, 0] = pick(core_ref, q[32:], q[:32]).reshape(4, 8, TILE)


EARLY = 8


def eliminate(both, first, last):
    tiles = [both[8 * t : 8 * t + 8] for t in range(8)]
    sub = lax.broadcasted_iota(jnp.int32, (8, 128), 0)
    for i in range(first, last):
        b, r = divmod(i, 8)
        pivot = tiles[b][r : r + 1]
        scaled = pivot * (1.0 / pivot[:, i : i + 1])
        for t in range(b, 8):
            factor = jnp.broadcast_to(tiles[t][:, i : i + 1], (8, 128))
            if t == b:
                factor = jnp.where(sub > r, factor, 0.0)
            tiles[t] = tiles[t] - factor * scaled
    return jnp.concatenate(tiles, axis=0)


def identity():
    row = lax.broadcasted_iota(jnp.int32, (K, K), 0)
    lane = lax.broadcasted_iota(jnp.int32, (K, K), 1)
    return jnp.where(row == lane, 1.0, 0.0)


def early_kernel(gram_ref, both_ref):
    both_ref[...] = eliminate(jnp.concatenate([gram_ref[...], identity()], axis=1), 0, EARLY)


def factor_kernel(both_ref, p_ref, linv_ref, pf_ref):
    both = eliminate(both_ref[...], EARLY, K)
    pivots = jnp.sum(both[:, :K] * identity(), axis=1, keepdims=True)
    linv = both[:, K:] * lax.rsqrt(pivots)
    linv_ref[...] = linv
    pf_ref[...] = dot(linv, p_ref[...], 1, 0, HI)


def place(grad_ref, z_ref, halves, value_ref):
    for slot, half in enumerate(halves):
        src = lax.rem(z_ref[0] + (NZ - half // 2), NZ) * 128 + (half % 2) * 64
        grad_ref[pl.ds(pl.multiple_of(src, 64), 64), :] = value_ref[
            64 * slot : 64 * (slot + 1)
        ].astype(BF16)


def accumulate(acc_ref, part):
    @pl.when(pl.program_id(0) == 0)
    def _():
        acc_ref[...] = part

    @pl.when(pl.program_id(0) > 0)
    def _():
        acc_ref[...] += part


def near_kernel(*refs):
    blocks = refs[:-6]
    a_ref, w_ref, sum_ref, merged_ref, grad_ref, acc_ref = refs[-6:]
    rows = jnp.concatenate([b[...] for b in blocks], axis=0)
    before = sum_ref[...].reshape(256, TILE).astype(F32)
    merged_ref[...] = before + jnp.dot(a_ref[...], rows, preferred_element_type=F32)
    accumulate(acc_ref, dot(rows, w_ref[...], 1, 1))

    @pl.when(pl.program_id(0) == pl.num_programs(0) - 1)
    def _():
        grad_ref[...] = acc_ref[...].astype(BF16)


def tail_kernel(z_ref, core_ref, *refs):
    blocks = refs[:4]
    a_ref, w_ref, sum_ref, first_ref, second_ref, mine_ref, other_ref, linv_ref, pf_ref = refs[4:13]
    err_ref, q_ref, grad_ref, acc_ref = refs[13:]
    mine = mine_ref[:, 0].reshape(32, TILE)
    other = other_ref[:, 0].reshape(32, TILE)
    raw = jnp.concatenate([pick(core_ref, mine, other), pick(core_ref, other, mine)], axis=0)
    qf = dot(linv_ref[...], raw, 1, 0, HI) * (1.0 / 32)
    q_ref[...] = qf
    pf = pf_ref[...]
    pf_hi = pf.astype(BF16)
    pf_lo = (pf - pf_hi.astype(F32)).astype(BF16)
    q_hi = qf.astype(BF16)
    q_lo = (qf - q_hi.astype(F32)).astype(BF16)
    low = dot(
        jnp.concatenate([pf_hi, pf_hi, pf_lo], axis=0),
        jnp.concatenate([q_hi, q_lo, q_hi], axis=0), 0, 0,
    )
    rows = jnp.concatenate([b[...] for b in blocks], axis=0)
    merged = sum_ref[...] + jnp.dot(a_ref[...], rows, preferred_element_type=F32)
    err_ref[0] = (merged - low).astype(BF16)
    accumulate(acc_ref, dot(rows, w_ref[...], 1, 1))

    @pl.when(pl.program_id(0) == pl.num_programs(0) - 1)
    def _():
        place(grad_ref, z_ref, FIRST, first_ref)
        place(grad_ref, z_ref, SECOND, second_ref)
        place(grad_ref, z_ref, FAR, acc_ref)


def shift(v, axis, size, by):
    return lax.ppermute(v, axis, [(i, (i + by) % size) for i in range(size)])


def on_device(grad_out, attn_out, out_weight, error_prev, q_prev):
    z = lax.axis_index("z").astype(jnp.int32).reshape(1)
    core = lax.axis_index("core").astype(jnp.int32).reshape(1)
    up = lambda v: shift(v, "z", NZ, 1)
    down = lambda v: shift(v, "z", NZ, NZ - 1)
    swap = lambda v: shift(v, "core", 2, 1)
    plane = lambda v: lax.all_to_all(v, ("x", "y"), 0, 0)
    column = lambda v: lax.all_to_all(v, "z", 0, 0)
    tied = lambda *v: lax.optimization_barrier(v)
    q_prev_t = q_prev.T
    tile = lambda rows: pl.BlockSpec((rows, TILE), lambda i: (0, i))
    err_tile = pl.BlockSpec((1, 256, TILE), lambda i: (0, 0, i))
    chunk_tile = pl.BlockSpec((4, 1, 8, TILE), lambda i: (0, i, 0, 0))
    chunks = (NXY, 8, TILE)

    specs = lambda blocks, a: [tile(v.shape[0]) for v in blocks] + [whole(a.shape), tile(256)]

    def near(blocks, a, before, before_spec):
        return call(
            near_kernel, [*blocks, a, out_weight, before], specs(blocks, a) + [before_spec],
            [out((256, D)), out((384, 256), BF16)], [tile(256), whole((384, 256))], grid=(NT,),
            scratch=[pltpu.VMEM((384, 256), F32)], mib=28, hbm_in=range(len(blocks) + 3),
            hbm_out=(0, 1),
        )

    (y,) = call(
        rows_kernel, [q_prev_t, grad_out], [tile(K), tile(128)], [out((NZ, K, 128))],
        [whole((NZ, K, 128))], grid=(NT,), scratch=[pltpu.VMEM((K, 128), F32)], hbm_in=(0, 1),
        hbm_out=(0,),
    )
    ga, gb = call(
        halves_kernel, [grad_out], [tile(128)], [out((64, D), BF16)] * 2, [tile(64)] * 2,
        grid=(NT,), hbm_in=(0,), hbm_out=(0, 1),
    )
    y = column(y)
    (eq_t,) = simple(error_rows_kernel, [q_prev_t, error_prev], [out((K, 256))], hbm_out=(0,))
    u1a, d1b = up(ga), down(gb)
    u1b, d1a = up(gb), down(ga)
    mine, other = simple(
        left_kernel, [core, y, attn_out, eq_t], [out((32, 256)), out((32, 256))], hbm_in=(2, 3)
    )
    (mine,) = simple(pair_kernel, [mine, swap(other)], [out((NXY, 32, 256))])
    mine, shadow = tied(mine, attn_out)
    mine = plane(mine)
    a_first, a_second, a_far = simple(
        turn_kernel, [z, shadow],
        [out((256, 384), BF16), out((256, 384), BF16), out((256, 256), BF16)],
    )
    a_first, u1a, d1b = tied(a_first, u1a, d1b)
    u2a, d2b = up(u1a), down(d1b)
    mine, a_first, a_second, a_far = tied(mine, a_first, a_second, a_far)
    (mine,) = simple(total_kernel, [mine], [out((32, 256))])

    p_t, sent = simple(
        terms_kernel, [core, mine, swap(mine), attn_out], [out((K, 256)), out((NZ, 96, 128))]
    )
    sent, p_t, a_first = tied(sent, p_t, a_first)
    got = column(sent)
    merged, grad_first = near([grad_out, u1a, u1b, d1a, d1b], a_first, error_prev, err_tile)
    p_then, u2a, d2b, u1b, d1a = tied(p_t, u2a, d2b, u1b, d1a)
    u2b, d2a = up(u1b), down(d1a)
    (ep,) = call(
        error_terms_kernel, [p_then, error_prev], [whole((K, 256)), err_tile], [out((K, D))],
        [tile(K)], grid=(NT,), flops=3 * 10**9,
    )
    got, merged, grad_first = tied(got, merged, grad_first)
    mine, other, gram = call(
        right_kernel, [core, got, ep, grad_out],
        [SMEM, whole((NZ, 96, 128)), tile(K), tile(128)],
        [out((4, NT, 8, TILE)), out((4, NT, 8, TILE)), out((K, K))],
        [chunk_tile, chunk_tile, whole((K, K))], grid=(NT,), hbm_in=(3,),
    )

    other = swap(other)
    (mine,) = simple(add_kernel, [mine.reshape(chunks), other.reshape(chunks)], [out(chunks)])
    mine, gram, p_t = tied(mine, gram, p_t)
    mine = plane(mine)
    (early,) = simple(early_kernel, [gram], [out((K, 128))])
    early, u2a, d2b = tied(early, u2a, d2b)
    u3a, d3b = up(u2a), down(d2b)
    linv, pf_t = simple(factor_kernel, [early, p_t], [out((K, K)), out((K, 256))])
    mine, linv, pf_t = tied(mine, linv, pf_t)
    (mine,) = simple(spread_kernel, [mine], [out((NZ, 8, TILE))])
    mine, u2b, d2a = tied(mine, u2b, d2a)
    mine = column(mine)
    u3b, d3a = up(u2b), down(d2a)
    far_a, far_b = up(u3a), down(d3b)
    (mine,) = simple(spread_kernel, [mine], [out(chunks)])
    mine, a_second, a_far, merged = tied(mine, a_second, a_far, merged)
    mine = plane(mine)
    merged, grad_second = near([u2a, u2b, u3a, d3b, d2a, d2b], a_second, merged, tile(256))
    linv, merged, u3b, far_a, far_b, d3a = tied(linv, merged, u3b, far_a, far_b, d3a)
    (linv,) = simple(copy_kernel, [linv], [out((K, K))])
    mine, linv, merged, grad_second = tied(mine, linv, merged, grad_second)
    other = swap(mine)
    far = [u3b, far_a, far_b, d3a]
    error_new, q_t, grad_attn = call(
        tail_kernel,
        [z, core, *far, a_far, out_weight, merged, grad_first, grad_second,
         mine.reshape(4, NT, 8, TILE), other.reshape(4, NT, 8, TILE), linv, pf_t],
        [SMEM, SMEM] + specs(far, a_far) + [tile(256), whole((384, 256)), whole((384, 256)),
         chunk_tile, chunk_tile, whole((K, K)), whole((K, 256))],
        [out((1, 256, D), BF16), out((K, D)), out((1024, 256), BF16)],
        [err_tile, tile(K), whole((1024, 256))], grid=(NT,),
        scratch=[pltpu.VMEM((256, 256), F32)], mib=28, hbm_in=range(2, 11), hbm_out=(0, 1, 2),
    )
    return grad_attn, pf_t.T, q_t.T, error_new


def solution(mesh):
    fine = Mesh(mesh.devices.reshape(4, 4, 2, 8), ("x", "y", "core", "z"))
    dp = ("x", "y", "core")
    in_specs = (P(dp + ("z",), None), P(dp, "z"), P("z", None), P(dp, "z", None), P())
    out_specs = (P(dp, "z"), P("z", None), P(), P(dp, "z", None))
    return jax.shard_map(
        on_device, mesh=fine, in_specs=in_specs, out_specs=out_specs, check_vma=False
    )
```
